256 devices in a mesh: chan: 64 (over z, y, core), row: 4 (over x).
Axes of the slice: x: 4, y: 4, z: 8, core: 2. Of those that a mesh axis runs over, the one named last changes fastest.
Arguments:
- counts: int32 [4, 64, 2048, 512], P('row', None, 'chan'), may hold values from 1 to 109, as said below
- template_mask: int32 [32, 2048], replicated, may hold values from 0 to 1, as said below
- weights_init: float32 [4, 64, 128, 512], P('row', 'chan'), may hold values from 0.05 to 0.5
- spectra_init: float32 [96, 2048], replicated, may hold values from 0.02 to 0.2
Outputs:
- weights: float32 [4, 64, 128, 512], P('row', 'chan')
- free_spectra: float32 [96, 2048], replicated
The draws below stay inside these ranges and needn't reach their ends.
Inputs may be any that keep to these rules, and one draw needn't show every extreme that they name: `counts`: some entries reach the largest value. Every row of template_mask holds at least one 1.
All inputs are finite; a program needn't handle non-finite values.
Results may differ from the reference program's by a relative error of at most 0.00105.
Values may be sent and summed in bfloat16 or wider, within the bound.
No kernel may reach another device: no remote copies, remote signals or barrier semaphores. Data moves between devices by JAX's collectives and lax.ppermute only.
A program may use at most 64 MiB of HBM per device.

```python
import math
import jax
import jax.numpy as jnp
from jax import lax

CH = 2048
FIXED = 32
FREE = 96
LINES = 64
COLS = 512
PASSES = 3
ITERS = 4
BLOCKS = 4
K = 128


def draw_counts(key, part):
    subkeys = jax.random.split(jax.random.fold_in(key, 7), 6)
    pixel_scale = jax.random.randint(subkeys[0], (BLOCKS, LINES, 1, COLS), 1, 13)
    scale_first = jax.random.randint(subkeys[1], (1, 1, CH, 1), 1, 13)
    scale_second = jax.random.randint(subkeys[2], (1, 1, CH, 1), 1, 13)
    layer_level = (jnp.arange(LINES, dtype=jnp.int32) * 4 // LINES).reshape(1, LINES, 1, 1)
    upper = pixel_scale * (scale_first * (3 - layer_level) + scale_second * layer_level) * (1 + layer_level) // 16 + 1
    values = 1 + jax.random.randint(subkeys[3], (BLOCKS, LINES, CH, COLS), 0, upper)
    half_rows = BLOCKS * LINES // 2
    order = jax.random.permutation(subkeys[4], BLOCKS * LINES).astype(jnp.int32)
    row_pair = (order // 2).reshape(BLOCKS, LINES, 1, 1)
    channel = jnp.arange(CH, dtype=jnp.int32).reshape(1, 1, CH, 1)
    spiked = channel % 2 == 1
    hot = spiked & (row_pair == channel // 2 % half_rows)
    hot_values = jax.random.randint(subkeys[5], (BLOCKS, LINES, CH, COLS), 100, 110)
    values = jnp.where(spiked, jnp.where(hot, hot_values, 1), values)
    return values.at[0, LINES - 1, 0, 0].set(109)


def draw_template_mask(key, part):
    subkeys = jax.random.split(jax.random.fold_in(key, 11), 2)
    line_hits = (jax.random.randint(subkeys[0], (FIXED, CH), 0, 16) == 0).astype(jnp.int32)
    center = jax.random.randint(subkeys[1], (FIXED, 1), 0, CH)
    center_hit = (jnp.arange(CH, dtype=jnp.int32)[None, :] == center).astype(jnp.int32)
    return jnp.maximum(line_hits, center_hit)


def steps_of(stream_key, dims, shards, low, high):
    def one(dim, parts):
        steps = jax.random.uniform(jax.random.fold_in(jax.random.fold_in(stream_key, 6), dim), (parts,), jnp.float32, low / len(shards), high / len(shards))
        return jnp.repeat(jnp.exp(steps), dims[dim] // parts).reshape((-1,) + (1,) * (len(dims) - dim - 1))

    factor_of = one(*shards[0])
    for cut in shards[1:]:
        factor_of = factor_of * one(*cut)
    return factor_of


def setup_inputs(seed: int = 0) -> dict:
    seeds = jax.random.split(jax.random.key(seed), 5)
    return {
        "counts": draw_counts(jax.random.fold_in(seeds[4], 71), 0),
        "template_mask": draw_template_mask(jax.random.fold_in(seeds[4], 71), 0),
        "weights_init": jnp.clip(jnp.exp(math.log(0.5) - 2.3025851 * jax.random.uniform(seeds[2], (BLOCKS, LINES, K, COLS), jnp.float32) ** steps_of(seeds[2], (BLOCKS, LINES, K, COLS), ((0, 4), (1, 64)), -0.2, 0.2)), 0.05, 0.5),
        "spectra_init": jnp.clip(jnp.exp(jax.random.uniform(seeds[3], (FREE, CH), jnp.float32, math.log(0.02), math.log(0.2))), 0.02, 0.2),
    }


def rounded(values):
    return lax.optimization_barrier(values.astype(jnp.bfloat16)).astype(jnp.float32)


def smooth_window(window):
    padded = jnp.pad(window, ((1, 1), (0, 0), (1, 1)))
    beside = padded[2:, :, 1:-1] + padded[:-2, :, 1:-1] + padded[1:-1, :, 2:] + padded[1:-1, :, :-2]
    return 0.4 * window + 0.15 * beside


def block_data(grid, row_start, group):
    total_rows = grid.shape[0]
    span = group + 2 * PASSES
    lower = jnp.clip(row_start - PASSES, 0, total_rows - span).astype(jnp.int32)
    window = lax.dynamic_slice_in_dim(grid, lower, span, 0).astype(jnp.float32)
    for repeat in range(PASSES):
        window = smooth_window(window)
    offset = (row_start - lower).astype(jnp.int32)
    return rounded(lax.dynamic_slice_in_dim(window, offset, group, 0))


def reference(counts, template_mask, weights_init, spectra_init):
    total_rows = BLOCKS * LINES
    group = 16
    grid = counts.reshape(total_rows, CH, COLS)
    template = template_mask.astype(jnp.float32)
    weights = weights_init.reshape(total_rows, K, COLS)
    free_spectra = spectra_init
    starts = (jnp.arange(total_rows // group) * group).astype(jnp.int32)
    for iteration in range(ITERS):
        spectra = jnp.concatenate([template, free_spectra], axis=0)
        spectra_wide = rounded(spectra)
        weight_den = jnp.sum(spectra, axis=1)

        def visit(carry, inputs):
            spec_num, spec_den = carry
            row_start, block_weights = inputs
            pixel_data = block_data(grid, row_start, group)
            intensity = jnp.einsum("kc,rkp->rcp", spectra_wide, rounded(block_weights))
            ratios = rounded(pixel_data / intensity)
            numerator = jnp.einsum("kc,rcp->rkp", spectra_wide, ratios)
            block_new = block_weights * numerator / weight_den[None, :, None]
            new_low = rounded(block_new)
            new_intensity = jnp.einsum("kc,rkp->rcp", spectra_wide, new_low)
            new_ratios = rounded(pixel_data / new_intensity)
            spec_num = spec_num + jnp.einsum("rkp,rcp->kc", new_low[:, FIXED:], new_ratios)
            spec_den = spec_den + jnp.sum(block_new[:, FIXED:], axis=(0, 2))
            return (spec_num, spec_den), block_new

        initial = (jnp.zeros((FREE, CH), jnp.float32), jnp.zeros((FREE,), jnp.float32))
        (spec_num, spec_den), blocks_new = lax.scan(visit, initial, (starts, weights.reshape(-1, group, K, COLS)))
        weights = blocks_new.reshape(total_rows, K, COLS)
        free_spectra = free_spectra * spec_num / spec_den[:, None]
    return weights.reshape(BLOCKS, LINES, K, COLS), free_spectra
```

```python
import jax
import jax.numpy as jnp
import numpy as np
from jax import lax
from jax.sharding import PartitionSpec as P

FIXED = 32
FREE = 96
PASSES = 3
ITERS = 4
CHAN = ("z", "y", "core")
PLANE = ("y", "row")
CORES = 2
HALF = FREE // CORES
LANES = 128


def with_rims(counts):
    size = lax.axis_size("row")
    up = [(i, i + 1) for i in range(size - 1)]
    down = [(j, i) for i, j in up]
    first = counts[:, :PASSES].astype(jnp.bfloat16)
    last = counts[:, -PASSES:].astype(jnp.bfloat16)
    before = lax.ppermute(last, "row", up)
    after = lax.ppermute(first, "row", down)
    parts = [before.astype(jnp.float32), counts.astype(jnp.float32), after.astype(jnp.float32)]
    return jnp.concatenate(parts, axis=1)


def smoothed(counts):
    field = with_rims(counts)
    lines = counts.shape[1]
    row, last = lax.axis_index("row"), lax.axis_size("row") - 1
    for step in range(PASSES):
        center = field[:, 1:-1]
        side = jnp.pad(center, ((0, 0), (0, 0), (0, 0), (1, 1)))
        beside = field[:, 2:] + field[:, :-2] + side[..., 2:] + side[..., :-2]
        field = 0.4 * center + 0.15 * beside
        rim = PASSES - 1 - step
        if rim:
            at = jnp.arange(lines + 2 * rim)
            inside = ((at >= rim) | (row > 0)) & ((at < lines + rim) | (row < last))
            field = jnp.where(inside[None, :, None, None], field, 0.0)
    return field.astype(jnp.bfloat16)


def to_all(x, axes):
    count = 1
    for axis in axes:
        count *= lax.axis_size(axis)
    return lax.all_to_all(jnp.broadcast_to(x[None], (count,) + x.shape), axes, 0, 0, tiled=True)


def summed_block(num, den):
    shards = num.shape[1] // LANES
    mine = lax.axis_index("core")
    blocks = num.reshape(CORES, HALF, shards, LANES).transpose(0, 2, 1, 3)
    rows = jnp.pad(den.reshape(CORES, 1, 1, HALF), ((0, 0), (0, 0), (0, 7), (0, LANES - HALF)))
    rows = jnp.broadcast_to(rows, (CORES, shards, 8, LANES))
    blocks = jnp.concatenate([blocks, rows], axis=2)
    kept = lax.dynamic_index_in_dim(blocks, mine, 0, keepdims=False)
    sent = lax.dynamic_index_in_dim(blocks, 1 - mine, 0, keepdims=False)
    chip = kept + lax.ppermute(sent, "core", [(0, 1), (1, 0)])
    plane = jnp.sum(lax.all_to_all(chip, PLANE, 0, 0, tiled=True), axis=0)
    total = jnp.sum(to_all(plane, ("z",)), axis=0)
    return total[:HALF], total[HALF, :HALF]


def gathered(block):
    halves = lax.all_gather(to_all(block, PLANE), "core")
    return halves.transpose(0, 2, 1, 3).reshape(FREE, -1)


def shards(counts, template_mask, weights_init, spectra_init):
    pixel_data = lax.all_to_all(smoothed(counts), CHAN, split_axis=1, concat_axis=2, tiled=True)[0]
    pixel_wide = pixel_data.astype(jnp.float32)
    weights = weights_init[0]
    template = template_mask.astype(jnp.float32)
    free_spectra = spectra_init
    shard = lax.axis_index("y") * lax.axis_size("row") + lax.axis_index("row")
    block = lax.dynamic_slice(
        spectra_init, (lax.axis_index("core") * HALF, shard * LANES), (HALF, LANES)
    )
    for iteration in range(ITERS):
        spectra = jnp.concatenate([template, free_spectra], axis=0)
        spectra_low = spectra.astype(jnp.bfloat16)
        weight_den = jnp.sum(spectra, axis=1)
        weight_low = weights.astype(jnp.bfloat16)
        intensity = jnp.einsum(
            "kc,lkp->lcp", spectra_low, weight_low, preferred_element_type=jnp.float32
        )
        ratios = (pixel_wide / intensity).astype(jnp.bfloat16)
        numerator = jnp.einsum(
            "kc,lcp->lkp", spectra_low, ratios, preferred_element_type=jnp.float32
        )
        weights = weights * numerator / weight_den[None, :, None]
        new_low = weights.astype(jnp.bfloat16)
        new_intensity = jnp.einsum(
            "kc,lkp->lcp", spectra_low, new_low, preferred_element_type=jnp.float32
        )
        new_ratios = (pixel_wide / new_intensity).astype(jnp.bfloat16)
        spec_num = jnp.einsum(
            "lkp,lcp->kc", new_low[:, FIXED:], new_ratios, preferred_element_type=jnp.float32
        )
        spec_den = jnp.sum(weights[:, FIXED:], axis=(0, 2))
        block_num, block_den = summed_block(spec_num, spec_den)
        block = block * block_num / block_den[:, None]
        free_spectra = gathered(block)
    return (weights[None], free_spectra)


def solution(mesh):
    devices = np.asarray(mesh.devices)
    fine = jax.sharding.Mesh(devices.reshape(8, 4, 2, 4), ("z", "y", "core", "row"))
    placed = (P("row", None, CHAN, None), P(), P("row", CHAN, None, None), P())
    return jax.shard_map(
        shards,
        mesh=fine,
        in_specs=placed,
        out_specs=(P("row", CHAN, None, None), P()),
        check_vma=False,
    )
```

```python
import jax
import jax.numpy as jnp
import numpy as np
from jax import lax
from jax.experimental import pallas as pl
from jax.experimental.pallas import tpu as pltpu
from jax.sharding import PartitionSpec as P

FIXED = 32
FREE = 96
PASSES = 3
ITERS = 4
CHAN = ("z", "y", "core")
PLANE = ("y", "row")
CORES = 2
HALF = FREE // CORES
LANES = 128
DEN_ROWS = 8
CHUNK = 256
VMEM = pl.BlockSpec(memory_space=pltpu.VMEM)
SMEM = pl.BlockSpec(memory_space=pltpu.SMEM)


def with_rims(counts):
    size = lax.axis_size("row")
    up = [(i, i + 1) for i in range(size - 1)]
    down = [(j, i) for i, j in up]
    first = counts[:, :PASSES].astype(jnp.bfloat16)
    last = counts[:, -PASSES:].astype(jnp.bfloat16)
    before = lax.ppermute(last, "row", up)
    after = lax.ppermute(first, "row", down)
    parts = [before.astype(jnp.float32), counts.astype(jnp.float32), after.astype(jnp.float32)]
    return jnp.concatenate(parts, axis=1)


def smoothed(counts):
    field = with_rims(counts)
    lines = counts.shape[1]
    row, last = lax.axis_index("row"), lax.axis_size("row") - 1
    for step in range(PASSES):
        center = field[:, 1:-1]
        side = jnp.pad(center, ((0, 0), (0, 0), (0, 0), (1, 1)))
        beside = field[:, 2:] + field[:, :-2] + side[..., 2:] + side[..., :-2]
        field = 0.4 * center + 0.15 * beside
        rim = PASSES - 1 - step
        if rim:
            at = jnp.arange(lines + 2 * rim)
            inside = ((at >= rim) | (row > 0)) & ((at < lines + rim) | (row < last))
            field = jnp.where(inside[None, :, None, None], field, 0.0)
    return field.astype(jnp.bfloat16)


def to_all(x, axes):
    count = 1
    for axis in axes:
        count *= lax.axis_size(axis)
    return lax.all_to_all(jnp.broadcast_to(x[None], (count,) + x.shape), axes, 0, 0, tiled=True)


def summed_block(kept, sent):
    chip = kept + lax.ppermute(sent, "core", [(0, 1), (1, 0)])
    plane = jnp.sum(lax.all_to_all(chip, PLANE, 0, 0, tiled=True), axis=0)
    total = jnp.sum(to_all(plane, ("z",)), axis=0)
    return total[:HALF], total[HALF, :HALF]


def update_kernel(core, data, template, halves, weights, new_weights, kept, sent, low, low_t):
    channels, pixels = data.shape
    shards = channels // LANES
    den = [jnp.sum(template[...].astype(jnp.float32), axis=1, keepdims=True)]
    low[:FIXED] = template[...]
    for half in range(CORES):
        rows = pl.ds(FIXED + half * HALF, HALF)
        total = jnp.zeros((HALF, LANES), jnp.float32)
        for shard in range(shards):
            part = halves[half, shard]
            total = total + part
            low[rows, pl.ds(shard * LANES, LANES)] = part.astype(jnp.bfloat16)
        den.append(jnp.sum(total, axis=1, keepdims=True))
    weight_den = jnp.concatenate(den, axis=0)
    for shard in range(shards):
        low_t[pl.ds(shard * LANES, LANES), :] = low[:, pl.ds(shard * LANES, LANES)].T

    old = weights[...]
    old_low = old.astype(jnp.bfloat16)

    def ratios_of(chunk, held):
        part = pl.ds(chunk * CHUNK, CHUNK)
        intensity = jnp.dot(low_t[part, :], held, preferred_element_type=jnp.float32)
        return (data[part, :].astype(jnp.float32) / intensity).astype(jnp.bfloat16)

    numerator = jnp.zeros(old.shape, jnp.float32)
    for chunk in range(channels // CHUNK):
        ratios = ratios_of(chunk, old_low)
        numerator += jnp.dot(
            low[:, pl.ds(chunk * CHUNK, CHUNK)], ratios, preferred_element_type=jnp.float32
        )
    new = old * numerator / weight_den
    new_weights[...] = new
    new_low = new.astype(jnp.bfloat16)
    mine = core[0]
    sums = jnp.sum(new[FIXED:], axis=1, keepdims=True)
    at = lax.broadcasted_iota(jnp.int32, (HALF, LANES), 0)
    lane = lax.broadcasted_iota(jnp.int32, (HALF, LANES), 1)
    den_rows = []
    for half in range(CORES):
        column = jnp.broadcast_to(sums[half * HALF : (half + 1) * HALF], (HALF, LANES))
        row = jnp.sum(jnp.where(at == lane, column, 0.0), axis=0, keepdims=True)
        den_rows.append(jnp.broadcast_to(row, (DEN_ROWS, LANES)))
    first = mine == 0
    kept_row = jnp.where(first, den_rows[0], den_rows[1])
    sent_row = jnp.where(first, den_rows[1], den_rows[0])
    for chunk in range(channels // CHUNK):
        ratios = ratios_of(chunk, new_low)
        terms = lax.dot_general(
            new_low[FIXED:], ratios, (((1,), (1,)), ((), ())), preferred_element_type=jnp.float32
        )
        for part in range(CHUNK // LANES):
            shard = chunk * (CHUNK // LANES) + part
            upper = terms[:HALF, part * LANES : (part + 1) * LANES]
            lower = terms[HALF:, part * LANES : (part + 1) * LANES]
            kept[shard, :HALF] = jnp.where(first, upper, lower)
            sent[shard, :HALF] = jnp.where(first, lower, upper)
            kept[shard, HALF:] = kept_row
            sent[shard, HALF:] = sent_row


def update(core, data, template, halves, weights):
    channels = data.shape[0]
    message = jax.ShapeDtypeStruct((channels // LANES, HALF + DEN_ROWS, LANES), jnp.float32)
    components = template.shape[0] + FREE
    return pl.pallas_call(
        update_kernel,
        out_shape=(jax.ShapeDtypeStruct(weights.shape, jnp.float32), message, message),
        in_specs=[SMEM, VMEM, VMEM, VMEM, VMEM],
        out_specs=(VMEM, VMEM, VMEM),
        scratch_shapes=[
            pltpu.VMEM((components, channels), jnp.bfloat16),
            pltpu.VMEM((channels, components), jnp.bfloat16),
        ],
        compiler_params=pltpu.CompilerParams(vmem_limit_bytes=32 * 1024 * 1024),
        name="update",
    )(core, data, template, halves, weights)


def shards(counts, template_mask, weights_init, spectra_init):
    pixel_data = lax.all_to_all(smoothed(counts), CHAN, split_axis=1, concat_axis=2, tiled=True)
    data = pixel_data.reshape(-1, pixel_data.shape[-1])
    core = lax.axis_index("core")
    template = template_mask.astype(jnp.bfloat16)
    weights = weights_init[0, 0]
    shard = lax.axis_index("y") * lax.axis_size("row") + lax.axis_index("row")
    halves = spectra_init.reshape(CORES, HALF, -1, LANES).transpose(0, 2, 1, 3)
    block = halves[core, shard]
    for iteration in range(ITERS):
        weights, kept, sent = update(core[None], data, template, halves, weights)
        num, den = summed_block(kept, sent)
        block = block * num / den[:, None]
        halves = lax.all_gather(to_all(block, PLANE), "core")
    free_spectra = halves.transpose(0, 2, 1, 3).reshape(FREE, -1)
    return (weights[None, None], free_spectra)


def solution(mesh):
    devices = np.asarray(mesh.devices)
    fine = jax.sharding.Mesh(devices.reshape(8, 4, 2, 4), ("z", "y", "core", "row"))
    placed = (P("row", None, CHAN, None), P(), P("row", CHAN, None, None), P())
    return jax.shard_map(
        shards,
        mesh=fine,
        in_specs=placed,
        out_specs=(P("row", CHAN, None, None), P()),
        check_vma=False,
    )
```

```python
import jax
import jax.numpy as jnp
import numpy as np
from jax import lax
from jax.experimental import pallas as pl
from jax.experimental.pallas import tpu as pltpu
from jax.sharding import PartitionSpec as P

FIXED = 32
FREE = 96
PASSES = 3
ITERS = 4
CHAN = ("z", "y", "core")
PLANE = ("y", "row")
CORES = 2
HALF = FREE // CORES
LANES = 128
DEN_ROWS = 8
CHUNK = 256
ROWS = 8
TAU = 8.0 / 3.0
SCALE = 0.15**3
VMEM = pl.BlockSpec(memory_space=pltpu.VMEM)
SMEM = pl.BlockSpec(memory_space=pltpu.SMEM)
ANY = pl.BlockSpec(memory_space=pl.ANY)


def column_sums(width):
    beside = np.eye(width, k=1) + np.eye(width, k=-1)
    powers = [3 * beside, 3 * beside @ beside, beside @ beside @ beside]
    return jnp.asarray(np.concatenate(powers, axis=1), jnp.bfloat16)


def beside_of(rows, sums):
    width = rows.shape[-1]
    flat = rows.reshape(-1, width).astype(jnp.bfloat16)
    out = jnp.dot(flat, sums, preferred_element_type=jnp.float32)
    return [out[:, at * width : (at + 1) * width].reshape(rows.shape) for at in range(PASSES)]


def inner_kernel(counts, sums, out, held, plain, beside, once, twice, done, in_sem, out_sem):
    lines = counts.shape[0]
    turns = lines // ROWS

    def fetch(turn):
        rows = pl.ds(turn * ROWS, ROWS)
        return pltpu.make_async_copy(counts.at[rows], held.at[rows], in_sem.at[turn])

    def ship(turn):
        start = turn * ROWS - PASSES
        return pltpu.make_async_copy(
            done.at[pl.ds(start + ROWS, ROWS)], out.at[pl.ds(start, ROWS)], out_sem.at[turn]
        )

    for turn in range(turns):
        fetch(turn).start()

    for turn in range(turns):
        fetch(turn).wait()
        base = turn * ROWS
        x = held[pl.ds(base, ROWS)].astype(jnp.float32)
        plain[pl.ds(base + ROWS, ROWS)] = x
        for at, value in enumerate(beside_of(x, sums[...])):
            beside[at, pl.ds(base + ROWS, ROWS)] = value
        for step, (source, target) in enumerate(((plain, once), (once, twice), (twice, done))):
            for row in range(ROWS):
                at = base + ROWS + row - step - 1
                value = TAU * source[at] + (source[at - 1] + source[at + 1]) + beside[step, at]
                if step == PASSES - 1:
                    value = (SCALE * value).astype(jnp.bfloat16)
                target[at] = value

        if turn:
            ship(turn).start()

    short = pltpu.make_async_copy(
        done.at[pl.ds(ROWS + PASSES, ROWS - 2 * PASSES)], out.at[pl.ds(PASSES, ROWS - 2 * PASSES)], out_sem.at[0]
    )
    short.start()
    short.wait()
    for turn in range(1, turns):
        ship(turn).wait()


def edge_kernel(flags, sums, counts_first, counts_last, before, after, inner, out, ends, sem):
    del inner
    lines = out.shape[0]
    copies = []
    for top in (True, False):
        near, rim = (counts_first, before) if top else (counts_last, after)
        pair = (rim[...], near[...]) if top else (near[...], rim[...])
        field = jnp.concatenate(pair, axis=0).astype(jnp.float32)
        beside = beside_of(field, sums[...])
        rows = [field[row] for row in range(3 * PASSES)]
        flag = flags[0] if top else flags[1]
        for step in range(PASSES):
            rows = [
                TAU * rows[row + 1] + (rows[row] + rows[row + 2]) + beside[step][row + 1 + step]
                for row in range(len(rows) - 2)
            ]
            beyond = PASSES - 1 - step
            for row in range(beyond):
                spot = row if top else len(rows) - 1 - row
                rows[spot] = rows[spot] * flag
        side = 0 if top else 1
        for row in range(PASSES):
            ends[side, row] = (SCALE * rows[row]).astype(jnp.bfloat16)
        target = out.at[pl.ds(0 if top else lines - PASSES, PASSES)]
        copies.append(pltpu.make_async_copy(ends.at[side], target, sem.at[side]))
        copies[-1].start()
    for copy in copies:
        copy.wait()


def smoothed(counts):
    lines, channels, width = counts.shape
    size, row = lax.axis_size("row"), lax.axis_index("row")
    up = [(i, i + 1) for i in range(size - 1)]
    down = [(j, i) for i, j in up]
    first, last = lax.optimization_barrier((counts[: 2 * PASSES], counts[-2 * PASSES :]))
    first, last = first.astype(jnp.bfloat16), last.astype(jnp.bfloat16)
    before = lax.ppermute(last[PASSES:], "row", up)
    after = lax.ppermute(first[:PASSES], "row", down)
    flags = jnp.stack([row > 0, row < size - 1]).astype(jnp.float32)
    shape = jax.ShapeDtypeStruct(counts.shape, jnp.bfloat16)
    sums = column_sums(width)
    padded = (lines + 2 * ROWS, channels, width)
    inner = pl.pallas_call(
        inner_kernel,
        out_shape=shape,
        in_specs=[ANY, VMEM],
        out_specs=ANY,
        scratch_shapes=[
            pltpu.VMEM(counts.shape, jnp.int32),
            pltpu.VMEM(padded, jnp.float32),
            pltpu.VMEM((PASSES,) + padded, jnp.float32),
            pltpu.VMEM(padded, jnp.float32),
            pltpu.VMEM(padded, jnp.float32),
            pltpu.VMEM(padded, jnp.bfloat16),
            pltpu.SemaphoreType.DMA((lines // ROWS,)),
            pltpu.SemaphoreType.DMA((lines // ROWS,)),
        ],
        compiler_params=pltpu.CompilerParams(vmem_limit_bytes=44 * 1024 * 1024),
        cost_estimate=pl.CostEstimate(
            flops=2 * lines * channels * width * width, bytes_accessed=6 * lines * channels * width, transcendentals=0
        ),
        name="smooth_inner",
    )(counts, sums)
    return pl.pallas_call(
        edge_kernel,
        out_shape=shape,
        in_specs=[SMEM, VMEM, VMEM, VMEM, VMEM, VMEM, ANY],
        out_specs=ANY,
        scratch_shapes=[
            pltpu.VMEM((2, PASSES, channels, width), jnp.bfloat16),
            pltpu.SemaphoreType.DMA((2,)),
        ],
        input_output_aliases={6: 0},
        compiler_params=pltpu.CompilerParams(vmem_limit_bytes=12 * 1024 * 1024),
        name="smooth_edges",
    )(flags, sums, first, last, before, after, inner)


def to_all(x, axes):
    count = 1
    for axis in axes:
        count *= lax.axis_size(axis)
    return lax.all_to_all(jnp.broadcast_to(x[None], (count,) + x.shape), axes, 0, 0, tiled=True)


def summed_block(kept, sent):
    chip = kept + lax.ppermute(sent, "core", [(0, 1), (1, 0)])
    plane = jnp.sum(lax.all_to_all(chip, PLANE, 0, 0, tiled=True), axis=0)
    total = jnp.sum(to_all(plane, ("z",)), axis=0)
    return total[:HALF], total[HALF, :HALF]


def update_kernel(core, data, template, own, other, weights, new_weights, kept, sent, low, low_t):
    channels, pixels = data.shape
    shards = channels // LANES
    mine = core[0]
    first = mine == 0
    den = []
    low[:FIXED] = template[...]
    for half, blocks in ((mine, own), (1 - mine, other)):
        rows = pl.ds(pl.multiple_of(FIXED + half * HALF, 16), HALF)
        total = jnp.zeros((HALF, LANES), jnp.float32)
        for shard in range(shards):
            part = blocks[shard]
            total = total + part
            low[rows, pl.ds(shard * LANES, LANES)] = part.astype(jnp.bfloat16)
        den.append(jnp.sum(total, axis=1, keepdims=True))
    upper, lower = jnp.where(first, den[0], den[1]), jnp.where(first, den[1], den[0])
    fixed = jnp.sum(template[...].astype(jnp.float32), axis=1, keepdims=True)
    weight_den = jnp.concatenate([fixed, upper, lower], axis=0)
    for shard in range(shards):
        low_t[pl.ds(shard * LANES, LANES), :] = low[:, pl.ds(shard * LANES, LANES)].T

    old = weights[...]
    old_low = old.astype(jnp.bfloat16)

    def ratios_of(chunk, held):
        part = pl.ds(chunk * CHUNK, CHUNK)
        intensity = jnp.dot(low_t[part, :], held, preferred_element_type=jnp.float32)
        return (data[part, :].astype(jnp.float32) / intensity).astype(jnp.bfloat16)

    numerator = jnp.zeros(old.shape, jnp.float32)
    for chunk in range(channels // CHUNK):
        ratios = ratios_of(chunk, old_low)
        numerator += jnp.dot(
            low[:, pl.ds(chunk * CHUNK, CHUNK)], ratios, preferred_element_type=jnp.float32
        )
    new = old * numerator / weight_den
    new_weights[...] = new
    new_low = new.astype(jnp.bfloat16)
    sums = jnp.sum(new[FIXED:], axis=1, keepdims=True)
    at = lax.broadcasted_iota(jnp.int32, (HALF, LANES), 0)
    lane = lax.broadcasted_iota(jnp.int32, (HALF, LANES), 1)
    den_rows = []
    for half in range(CORES):
        column = jnp.broadcast_to(sums[half * HALF : (half + 1) * HALF], (HALF, LANES))
        row = jnp.sum(jnp.where(at == lane, column, 0.0), axis=0, keepdims=True)
        den_rows.append(jnp.broadcast_to(row, (DEN_ROWS, LANES)))
    kept_row = jnp.where(first, den_rows[0], den_rows[1])
    sent_row = jnp.where(first, den_rows[1], den_rows[0])
    for chunk in range(channels // CHUNK):
        ratios = ratios_of(chunk, new_low)
        terms = lax.dot_general(
            new_low[FIXED:], ratios, (((1,), (1,)), ((), ())), preferred_element_type=jnp.float32
        )
        for part in range(CHUNK // LANES):
            shard = chunk * (CHUNK // LANES) + part
            upper = terms[:HALF, part * LANES : (part + 1) * LANES]
            lower = terms[HALF:, part * LANES : (part + 1) * LANES]
            kept[shard, :HALF] = jnp.where(first, upper, lower)
            sent[shard, :HALF] = jnp.where(first, lower, upper)
            kept[shard, HALF:] = kept_row
            sent[shard, HALF:] = sent_row


def update(core, data, template, own, other, weights):
    channels = data.shape[0]
    message = jax.ShapeDtypeStruct((channels // LANES, HALF + DEN_ROWS, LANES), jnp.float32)
    components = template.shape[0] + FREE
    return pl.pallas_call(
        update_kernel,
        out_shape=(jax.ShapeDtypeStruct(weights.shape, jnp.float32), message, message),
        in_specs=[SMEM, VMEM, VMEM, VMEM, VMEM, VMEM],
        out_specs=(VMEM, VMEM, VMEM),
        scratch_shapes=[
            pltpu.VMEM((components, channels), jnp.bfloat16),
            pltpu.VMEM((channels, components), jnp.bfloat16),
        ],
        compiler_params=pltpu.CompilerParams(vmem_limit_bytes=16 * 1024 * 1024),
        name="update",
    )(core, data, template, own, other, weights)


def whole_kernel(core, own, other, out):
    for half, blocks in ((core[0], own), (1 - core[0], other)):
        rows = pl.ds(pl.multiple_of(half * HALF, 8), HALF)
        for shard in range(blocks.shape[0]):
            out[rows, pl.ds(shard * LANES, LANES)] = blocks[shard]


def whole(core, own, other):
    return pl.pallas_call(
        whole_kernel,
        out_shape=jax.ShapeDtypeStruct((FREE, own.shape[0] * LANES), jnp.float32),
        in_specs=[SMEM, VMEM, VMEM],
        out_specs=VMEM,
        name="whole",
    )(core, own, other)


def shards(counts, template_mask, weights_init, spectra_init):
    pixel_data = lax.all_to_all(smoothed(counts[0]), CHAN, split_axis=0, concat_axis=0, tiled=True)
    data = pixel_data.reshape(-1, pixel_data.shape[-1])
    core = lax.axis_index("core")
    template = template_mask.astype(jnp.bfloat16)
    weights = weights_init[0, 0]
    shard = lax.axis_index("y") * lax.axis_size("row") + lax.axis_index("row")
    halves = spectra_init.reshape(CORES, HALF, -1, LANES).transpose(0, 2, 1, 3)
    own, other = halves[core], halves[1 - core]
    block = own[shard]
    for iteration in range(ITERS):
        weights, kept, sent = update(core[None], data, template, own, other, weights)
        num, den = summed_block(kept, sent)
        block = block * num / den[:, None]
        own = to_all(block, PLANE)
        other = lax.ppermute(own, "core", [(0, 1), (1, 0)])
    return (weights[None, None], whole(core[None], own, other))


def solution(mesh):
    devices = np.asarray(mesh.devices)
    fine = jax.sharding.Mesh(devices.reshape(8, 4, 2, 4), ("z", "y", "core", "row"))
    placed = (P("row", None, CHAN, None), P(), P("row", CHAN, None, None), P())
    return jax.shard_map(
        shards,
        mesh=fine,
        in_specs=placed,
        out_specs=(P("row", CHAN, None, None), P()),
        check_vma=False,
    )
```

```python
import jax
import jax.numpy as jnp
import numpy as np
from jax import lax
from jax.experimental import pallas as pl
from jax.experimental.pallas import tpu as pltpu
from jax.sharding import PartitionSpec as P

FIXED = 32
FREE = 96
PASSES = 3
ITERS = 4
CHAN = ("z", "y", "core")
PLANE = ("y", "row")
CORES = 2
HALF = FREE // CORES
LANES = 128
DEN_ROWS = 8
CHUNK = 256
ROWS = 8
INNER_MIB = 60
EDGE_MIB = 53
TAU = 8.0 / 3.0
SCALE = 0.15**3
VMEM = pl.BlockSpec(memory_space=pltpu.VMEM)
SMEM = pl.BlockSpec(memory_space=pltpu.SMEM)
HBM = pl.BlockSpec(memory_space=pltpu.HBM)


def column_sums(width):
    row = lax.broadcasted_iota(jnp.int32, (width, width), 0)
    column = lax.broadcasted_iota(jnp.int32, (width, width), 1)
    apart, total = jnp.abs(row - column), row + column
    corner = (total == 0) | (total == 2 * width - 2)
    beside_corner = (total == 1) | (total == 2 * width - 3)
    first = jnp.where(apart == 1, 3.0, 0.0)
    second = jnp.where(apart == 2, 3.0, jnp.where(apart == 0, jnp.where(corner, 3.0, 6.0), 0.0))
    third = jnp.where(apart == 3, 1.0, jnp.where(apart == 1, jnp.where(beside_corner, 2.0, 3.0), 0.0))
    return [power.astype(jnp.bfloat16) for power in (first, second, third)]


def fill_sums(sums):
    width = sums.shape[0]
    for at, power in enumerate(column_sums(width)):
        sums[:, pl.ds(at * width, width)] = power


def beside_of(rows, sums):
    width = rows.shape[-1]
    flat = rows.reshape(-1, width).astype(jnp.bfloat16)
    out = jnp.dot(flat, sums, preferred_element_type=jnp.float32)
    return [out[:, at * width : (at + 1) * width].reshape(rows.shape) for at in range(PASSES)]


def inner_kernel(counts, out, sums, held, plain, beside, once, twice, done, in_sem, out_sem):
    lines = counts.shape[0]
    turns = lines // ROWS

    def fetch(turn):
        rows = pl.ds(turn * ROWS, ROWS)
        return pltpu.make_async_copy(counts.at[rows], held.at[rows], in_sem.at[turn])

    def ship(turn):
        start = turn * ROWS - PASSES
        return pltpu.make_async_copy(
            done.at[pl.ds(start + ROWS, ROWS)], out.at[pl.ds(start, ROWS)], out_sem.at[turn]
        )

    for turn in range(turns):
        fetch(turn).start()
    fill_sums(sums)

    for turn in range(turns):
        fetch(turn).wait()
        base = turn * ROWS
        x = held[pl.ds(base, ROWS)].astype(jnp.float32)
        plain[pl.ds(base + ROWS, ROWS)] = x
        for at, value in enumerate(beside_of(x, sums[...])):
            beside[at, pl.ds(base + ROWS, ROWS)] = value
        for step, (source, target) in enumerate(((plain, once), (once, twice), (twice, done))):
            for row in range(ROWS):
                at = base + ROWS + row - step - 1
                value = TAU * source[at] + (source[at - 1] + source[at + 1]) + beside[step, at]
                if step == PASSES - 1:
                    value = (SCALE * value).astype(jnp.bfloat16)
                target[at] = value

        if turn:
            ship(turn).start()

    short = pltpu.make_async_copy(
        done.at[pl.ds(ROWS + PASSES, ROWS - 2 * PASSES)], out.at[pl.ds(PASSES, ROWS - 2 * PASSES)], out_sem.at[0]
    )
    short.start()
    short.wait()
    for turn in range(1, turns):
        ship(turn).wait()


def edge_kernel(flags, counts, before, after, inner, out, sums, near, rim, ends, in_sem, sem):
    del inner
    lines = out.shape[0]
    rows = 2 * PASSES
    fetches = [
        pltpu.make_async_copy(counts.at[pl.ds(0, rows)], near.at[0], in_sem.at[0]),
        pltpu.make_async_copy(counts.at[pl.ds(lines - rows, rows)], near.at[1], in_sem.at[1]),
        pltpu.make_async_copy(before, rim.at[0], in_sem.at[2]),
        pltpu.make_async_copy(after, rim.at[1], in_sem.at[3]),
    ]
    for fetch in fetches:
        fetch.start()
    fill_sums(sums)
    for fetch in fetches:
        fetch.wait()
    copies = []
    for top in (True, False):
        side = 0 if top else 1
        own, beyond = near[side].astype(jnp.float32), rim[side].astype(jnp.float32)
        pair = (beyond, own) if top else (own, beyond)
        field = jnp.concatenate(pair, axis=0)
        beside = beside_of(field, sums[...])
        rows = [field[row] for row in range(3 * PASSES)]
        flag = flags[0] if top else flags[1]
        for step in range(PASSES):
            rows = [
                TAU * rows[row + 1] + (rows[row] + rows[row + 2]) + beside[step][row + 1 + step]
                for row in range(len(rows) - 2)
            ]
            beyond = PASSES - 1 - step
            for row in range(beyond):
                spot = row if top else len(rows) - 1 - row
                rows[spot] = rows[spot] * flag
        for row in range(PASSES):
            ends[side, row] = (SCALE * rows[row]).astype(jnp.bfloat16)
        target = out.at[pl.ds(0 if top else lines - PASSES, PASSES)]
        copies.append(pltpu.make_async_copy(ends.at[side], target, sem.at[side]))
        copies[-1].start()
    for copy in copies:
        copy.wait()


def smoothed(counts):
    lines, channels, width = counts.shape
    size, row = lax.axis_size("row"), lax.axis_index("row")
    up = [(i, i + 1) for i in range(size - 1)]
    down = [(j, i) for i, j in up]
    first, last = lax.optimization_barrier((counts[:PASSES], counts[-PASSES:]))
    before = lax.ppermute(last.astype(jnp.bfloat16), "row", up)
    after = lax.ppermute(first.astype(jnp.bfloat16), "row", down)
    flags = jnp.stack([row > 0, row < size - 1]).astype(jnp.float32)
    shape = jax.ShapeDtypeStruct(counts.shape, jnp.bfloat16)
    padded = (lines + 2 * ROWS, channels, width)
    sums = pltpu.VMEM((width, PASSES * width), jnp.bfloat16)
    inner = pl.pallas_call(
        inner_kernel,
        out_shape=shape,
        in_specs=[HBM],
        out_specs=HBM,
        scratch_shapes=[
            sums,
            pltpu.VMEM(counts.shape, jnp.int32),
            pltpu.VMEM(padded, jnp.float32),
            pltpu.VMEM((PASSES,) + padded, jnp.float32),
            pltpu.VMEM(padded, jnp.float32),
            pltpu.VMEM(padded, jnp.float32),
            pltpu.VMEM(padded, jnp.bfloat16),
            pltpu.SemaphoreType.DMA((lines // ROWS,)),
            pltpu.SemaphoreType.DMA((lines // ROWS,)),
        ],
        compiler_params=pltpu.CompilerParams(vmem_limit_bytes=INNER_MIB * 1024 * 1024),
        cost_estimate=pl.CostEstimate(
            flops=2 * lines * channels * width * width, bytes_accessed=6 * lines * channels * width, transcendentals=0
        ),
        name="smooth_inner",
    )(counts)
    return pl.pallas_call(
        edge_kernel,
        out_shape=shape,
        in_specs=[SMEM, HBM, HBM, HBM, HBM],
        out_specs=HBM,
        scratch_shapes=[
            sums,
            pltpu.VMEM((2, 2 * PASSES, channels, width), jnp.int32),
            pltpu.VMEM((2, PASSES, channels, width), jnp.bfloat16),
            pltpu.VMEM((2, PASSES, channels, width), jnp.bfloat16),
            pltpu.SemaphoreType.DMA((4,)),
            pltpu.SemaphoreType.DMA((2,)),
        ],
        input_output_aliases={4: 0},
        compiler_params=pltpu.CompilerParams(vmem_limit_bytes=EDGE_MIB * 1024 * 1024),
        name="smooth_edges",
    )(flags, counts, before, after, inner)


def to_all(x, axes):
    count = 1
    for axis in axes:
        count *= lax.axis_size(axis)
    return lax.all_to_all(jnp.broadcast_to(x[None], (count,) + x.shape), axes, 0, 0, tiled=True)


def summed_block(kept, sent):
    chip = kept + lax.ppermute(sent, "core", [(0, 1), (1, 0)])
    plane = jnp.sum(lax.all_to_all(chip, PLANE, 0, 0, tiled=True), axis=0)
    total = jnp.sum(to_all(plane, ("z",)), axis=0)
    return total[:HALF], total[HALF, :HALF]


def update_kernel(core, data, template, own, other, weights, new_weights, kept, sent, low, low_t):
    channels, pixels = data.shape
    shards = channels // LANES
    mine = core[0]
    first = mine == 0
    den = []
    low[:FIXED] = template[...]
    for half, blocks in ((mine, own), (1 - mine, other)):
        rows = pl.ds(pl.multiple_of(FIXED + half * HALF, 16), HALF)
        total = jnp.zeros((HALF, LANES), jnp.float32)
        for shard in range(shards):
            part = blocks[shard]
            total = total + part
            low[rows, pl.ds(shard * LANES, LANES)] = part.astype(jnp.bfloat16)
        den.append(jnp.sum(total, axis=1, keepdims=True))
    upper, lower = jnp.where(first, den[0], den[1]), jnp.where(first, den[1], den[0])
    fixed = jnp.sum(template[...].astype(jnp.float32), axis=1, keepdims=True)
    weight_den = jnp.concatenate([fixed, upper, lower], axis=0)
    for shard in range(shards):
        low_t[pl.ds(shard * LANES, LANES), :] = low[:, pl.ds(shard * LANES, LANES)].T

    old = weights[...]
    old_low = old.astype(jnp.bfloat16)

    def ratios_of(chunk, held):
        part = pl.ds(chunk * CHUNK, CHUNK)
        intensity = jnp.dot(low_t[part, :], held, preferred_element_type=jnp.float32)
        return (data[part, :].astype(jnp.float32) / intensity).astype(jnp.bfloat16)

    numerator = jnp.zeros(old.shape, jnp.float32)
    for chunk in range(channels // CHUNK):
        ratios = ratios_of(chunk, old_low)
        numerator += jnp.dot(
            low[:, pl.ds(chunk * CHUNK, CHUNK)], ratios, preferred_element_type=jnp.float32
        )
    new = old * numerator / weight_den
    new_weights[...] = new
    new_low = new.astype(jnp.bfloat16)
    sums = jnp.sum(new[FIXED:], axis=1, keepdims=True)
    at = lax.broadcasted_iota(jnp.int32, (HALF, LANES), 0)
    lane = lax.broadcasted_iota(jnp.int32, (HALF, LANES), 1)
    den_rows = []
    for half in range(CORES):
        column = jnp.broadcast_to(sums[half * HALF : (half + 1) * HALF], (HALF, LANES))
        row = jnp.sum(jnp.where(at == lane, column, 0.0), axis=0, keepdims=True)
        den_rows.append(jnp.broadcast_to(row, (DEN_ROWS, LANES)))
    kept_row = jnp.where(first, den_rows[0], den_rows[1])
    sent_row = jnp.where(first, den_rows[1], den_rows[0])
    for chunk in range(channels // CHUNK):
        ratios = ratios_of(chunk, new_low)
        terms = lax.dot_general(
            new_low[FIXED:], ratios, (((1,), (1,)), ((), ())), preferred_element_type=jnp.float32
        )
        for part in range(CHUNK // LANES):
            shard = chunk * (CHUNK // LANES) + part
            upper = terms[:HALF, part * LANES : (part + 1) * LANES]
            lower = terms[HALF:, part * LANES : (part + 1) * LANES]
            kept[shard, :HALF] = jnp.where(first, upper, lower)
            sent[shard, :HALF] = jnp.where(first, lower, upper)
            kept[shard, HALF:] = kept_row
            sent[shard, HALF:] = sent_row


def update(core, data, template, own, other, weights):
    channels = data.shape[0]
    message = jax.ShapeDtypeStruct((channels // LANES, HALF + DEN_ROWS, LANES), jnp.float32)
    components = template.shape[0] + FREE
    return pl.pallas_call(
        update_kernel,
        out_shape=(jax.ShapeDtypeStruct(weights.shape, jnp.float32), message, message),
        in_specs=[SMEM, VMEM, VMEM, VMEM, VMEM, VMEM],
        out_specs=(VMEM, VMEM, VMEM),
        scratch_shapes=[
            pltpu.VMEM((components, channels), jnp.bfloat16),
            pltpu.VMEM((channels, components), jnp.bfloat16),
        ],
        compiler_params=pltpu.CompilerParams(vmem_limit_bytes=16 * 1024 * 1024),
        name="update",
    )(core, data, template, own, other, weights)


def whole_kernel(core, own, other, out):
    for half, blocks in ((core[0], own), (1 - core[0], other)):
        rows = pl.ds(pl.multiple_of(half * HALF, 8), HALF)
        for shard in range(blocks.shape[0]):
            out[rows, pl.ds(shard * LANES, LANES)] = blocks[shard]


def whole(core, own, other):
    return pl.pallas_call(
        whole_kernel,
        out_shape=jax.ShapeDtypeStruct((FREE, own.shape[0] * LANES), jnp.float32),
        in_specs=[SMEM, VMEM, VMEM],
        out_specs=VMEM,
        name="whole",
    )(core, own, other)


def shards(counts, template_mask, weights_init, spectra_init):
    pixel_data = lax.all_to_all(smoothed(counts[0]), CHAN, split_axis=0, concat_axis=0, tiled=True)
    data = pixel_data.reshape(-1, pixel_data.shape[-1])
    core = lax.axis_index("core")
    template = template_mask.astype(jnp.bfloat16)
    weights = weights_init[0, 0]
    shard = lax.axis_index("y") * lax.axis_size("row") + lax.axis_index("row")
    halves = spectra_init.reshape(CORES, HALF, -1, LANES).transpose(0, 2, 1, 3)
    own, other = halves[core], halves[1 - core]
    own, other, block = lax.optimization_barrier((own, other, own[shard]))
    for iteration in range(ITERS):
        weights, kept, sent = update(core[None], data, template, own, other, weights)
        num, den = summed_block(kept, sent)
        block = block * num / den[:, None]
        own = to_all(block, PLANE)
        other = lax.ppermute(own, "core", [(0, 1), (1, 0)])
    return (weights[None, None], whole(core[None], own, other))


def solution(mesh):
    devices = np.asarray(mesh.devices)
    fine = jax.sharding.Mesh(devices.reshape(8, 4, 2, 4), ("z", "y", "core", "row"))
    placed = (P("row", None, CHAN, None), P(), P("row", CHAN, None, None), P())
    return jax.shard_map(
        shards,
        mesh=fine,
        in_specs=placed,
        out_specs=(P("row", CHAN, None, None), P()),
        check_vma=False,
    )
```

```python
import jax
import jax.numpy as jnp
import numpy as np
from jax import lax
from jax.experimental import pallas as pl
from jax.experimental.pallas import tpu as pltpu
from jax.sharding import PartitionSpec as P

FIXED = 32
FREE = 96
PASSES = 3
ITERS = 4
CHAN = ("z", "y", "core")
PLANE = ("y", "row")
CORES = 2
HALF = FREE // CORES
LANES = 128
DEN_ROWS = 8
CHUNK = 256
ROWS = 8
INNER_MIB = 60
EDGE_MIB = 53
TAU = 8.0 / 3.0
SCALE = 0.15**3
VMEM = pl.BlockSpec(memory_space=pltpu.VMEM)
SMEM = pl.BlockSpec(memory_space=pltpu.SMEM)
HBM = pl.BlockSpec(memory_space=pltpu.HBM)


def column_sums(width):
    row = lax.broadcasted_iota(jnp.int32, (width, width), 0)
    column = lax.broadcasted_iota(jnp.int32, (width, width), 1)
    apart, total = jnp.abs(row - column), row + column
    corner = (total == 0) | (total == 2 * width - 2)
    beside_corner = (total == 1) | (total == 2 * width - 3)
    first = jnp.where(apart == 1, 3.0, 0.0)
    second = jnp.where(apart == 2, 3.0, jnp.where(apart == 0, jnp.where(corner, 3.0, 6.0), 0.0))
    third = jnp.where(apart == 3, 1.0, jnp.where(apart == 1, jnp.where(beside_corner, 2.0, 3.0), 0.0))
    return [power.astype(jnp.bfloat16) for power in (first, second, third)]


def fill_sums(sums):
    width = sums.shape[0]
    for at, power in enumerate(column_sums(width)):
        sums[:, pl.ds(at * width, width)] = power


def beside_of(rows, sums):
    width = rows.shape[-1]
    flat = rows.reshape(-1, width).astype(jnp.bfloat16)
    out = jnp.dot(flat, sums, preferred_element_type=jnp.float32)
    return [out[:, at * width : (at + 1) * width].reshape(rows.shape) for at in range(PASSES)]


def inner_kernel(counts, out, sums, held, plain, beside, once, twice, done, in_sem, out_sem):
    lines = counts.shape[0]
    turns = lines // ROWS

    def fetch(turn):
        rows = pl.ds(turn * ROWS, ROWS)
        return pltpu.make_async_copy(counts.at[rows], held.at[rows], in_sem.at[turn])

    def ship(turn):
        start = turn * ROWS - PASSES
        return pltpu.make_async_copy(
            done.at[pl.ds(start + ROWS, ROWS)], out.at[pl.ds(start, ROWS)], out_sem.at[turn]
        )

    for turn in range(turns):
        fetch(turn).start()
    fill_sums(sums)

    for turn in range(turns):
        fetch(turn).wait()
        base = turn * ROWS
        x = held[pl.ds(base, ROWS)].astype(jnp.float32)
        plain[pl.ds(base + ROWS, ROWS)] = x
        for at, value in enumerate(beside_of(x, sums[...])):
            beside[at, pl.ds(base + ROWS, ROWS)] = value
        for step, (source, target) in enumerate(((plain, once), (once, twice), (twice, done))):
            for row in range(ROWS):
                at = base + ROWS + row - step - 1
                value = TAU * source[at] + (source[at - 1] + source[at + 1]) + beside[step, at]
                if step == PASSES - 1:
                    value = (SCALE * value).astype(jnp.bfloat16)
                target[at] = value

        if turn:
            ship(turn).start()

    short = pltpu.make_async_copy(
        done.at[pl.ds(ROWS + PASSES, ROWS - 2 * PASSES)], out.at[pl.ds(PASSES, ROWS - 2 * PASSES)], out_sem.at[0]
    )
    short.start()
    short.wait()
    for turn in range(1, turns):
        ship(turn).wait()


def edge_kernel(flags, counts, before, after, inner, out, sums, near, rim, ends, in_sem, sem):
    del inner
    lines = out.shape[0]
    rows = 2 * PASSES
    fetches = [
        pltpu.make_async_copy(counts.at[pl.ds(0, rows)], near.at[0], in_sem.at[0]),
        pltpu.make_async_copy(counts.at[pl.ds(lines - rows, rows)], near.at[1], in_sem.at[1]),
        pltpu.make_async_copy(before, rim.at[0], in_sem.at[2]),
        pltpu.make_async_copy(after, rim.at[1], in_sem.at[3]),
    ]
    for fetch in fetches:
        fetch.start()
    fill_sums(sums)
    for fetch in fetches:
        fetch.wait()
    copies = []
    for top in (True, False):
        side = 0 if top else 1
        own, beyond = near[side].astype(jnp.float32), rim[side].astype(jnp.float32)
        pair = (beyond, own) if top else (own, beyond)
        field = jnp.concatenate(pair, axis=0)
        beside = beside_of(field, sums[...])
        rows = [field[row] for row in range(3 * PASSES)]
        flag = flags[0] if top else flags[1]
        for step in range(PASSES):
            rows = [
                TAU * rows[row + 1] + (rows[row] + rows[row + 2]) + beside[step][row + 1 + step]
                for row in range(len(rows) - 2)
            ]
            beyond = PASSES - 1 - step
            for row in range(beyond):
                spot = row if top else len(rows) - 1 - row
                rows[spot] = rows[spot] * flag
        for row in range(PASSES):
            ends[side, row] = (SCALE * rows[row]).astype(jnp.bfloat16)
        target = out.at[pl.ds(0 if top else lines - PASSES, PASSES)]
        copies.append(pltpu.make_async_copy(ends.at[side], target, sem.at[side]))
        copies[-1].start()
    for copy in copies:
        copy.wait()


def smoothed(counts):
    lines, channels, width = counts.shape
    size, row = lax.axis_size("row"), lax.axis_index("row")
    up = [(i, i + 1) for i in range(size - 1)]
    down = [(j, i) for i, j in up]
    first, last = lax.optimization_barrier((counts[:PASSES], counts[-PASSES:]))
    before = lax.ppermute(last.astype(jnp.bfloat16), "row", up)
    after = lax.ppermute(first.astype(jnp.bfloat16), "row", down)
    flags = jnp.stack([row > 0, row < size - 1]).astype(jnp.float32)
    shape = jax.ShapeDtypeStruct(counts.shape, jnp.bfloat16)
    padded = (lines + 2 * ROWS, channels, width)
    sums = pltpu.VMEM((width, PASSES * width), jnp.bfloat16)
    inner = pl.pallas_call(
        inner_kernel,
        out_shape=shape,
        in_specs=[HBM],
        out_specs=HBM,
        scratch_shapes=[
            sums,
            pltpu.VMEM(counts.shape, jnp.int32),
            pltpu.VMEM(padded, jnp.float32),
            pltpu.VMEM((PASSES,) + padded, jnp.float32),
            pltpu.VMEM(padded, jnp.float32),
            pltpu.VMEM(padded, jnp.float32),
            pltpu.VMEM(padded, jnp.bfloat16),
            pltpu.SemaphoreType.DMA((lines // ROWS,)),
            pltpu.SemaphoreType.DMA((lines // ROWS,)),
        ],
        compiler_params=pltpu.CompilerParams(vmem_limit_bytes=INNER_MIB * 1024 * 1024),
        cost_estimate=pl.CostEstimate(
            flops=2 * lines * channels * width * width, bytes_accessed=6 * lines * channels * width, transcendentals=0
        ),
        name="smooth_inner",
    )(counts)
    return pl.pallas_call(
        edge_kernel,
        out_shape=shape,
        in_specs=[SMEM, HBM, HBM, HBM, HBM],
        out_specs=HBM,
        scratch_shapes=[
            sums,
            pltpu.VMEM((2, 2 * PASSES, channels, width), jnp.int32),
            pltpu.VMEM((2, PASSES, channels, width), jnp.bfloat16),
            pltpu.VMEM((2, PASSES, channels, width), jnp.bfloat16),
            pltpu.SemaphoreType.DMA((4,)),
            pltpu.SemaphoreType.DMA((2,)),
        ],
        input_output_aliases={4: 0},
        compiler_params=pltpu.CompilerParams(vmem_limit_bytes=EDGE_MIB * 1024 * 1024),
        name="smooth_edges",
    )(flags, counts, before, after, inner)


def to_all(x, axes):
    count = 1
    for axis in axes:
        count *= lax.axis_size(axis)
    return lax.all_to_all(jnp.broadcast_to(x[None], (count,) + x.shape), axes, 0, 0, tiled=True)


def summed_block(kept, sent):
    chip = kept + lax.ppermute(sent, "core", [(0, 1), (1, 0)])
    plane = jnp.sum(lax.all_to_all(chip, PLANE, 0, 0, tiled=True), axis=0)
    total = jnp.sum(to_all(plane, ("z",)), axis=0)
    return total[:HALF], total[HALF, :HALF]


def update_kernel(core, data, template, own, other, weights, new_weights, kept, sent, low, low_t):
    channels, pixels = data.shape
    shards = channels // LANES
    mine = core[0]
    first = mine == 0
    den = []
    low[:FIXED] = template[...]
    for half, blocks in ((mine, own), (1 - mine, other)):
        rows = pl.ds(pl.multiple_of(FIXED + half * HALF, 16), HALF)
        total = jnp.zeros((HALF, LANES), jnp.float32)
        for shard in range(shards):
            part = blocks[shard]
            total = total + part
            low[rows, pl.ds(shard * LANES, LANES)] = part.astype(jnp.bfloat16)
        den.append(jnp.sum(total, axis=1, keepdims=True))
    upper, lower = jnp.where(first, den[0], den[1]), jnp.where(first, den[1], den[0])
    fixed = jnp.sum(template[...].astype(jnp.float32), axis=1, keepdims=True)
    weight_den = jnp.concatenate([fixed, upper, lower], axis=0)
    for shard in range(shards):
        low_t[pl.ds(shard * LANES, LANES), :] = low[:, pl.ds(shard * LANES, LANES)].T

    old = weights[...]
    old_low = old.astype(jnp.bfloat16)

    def ratios_of(chunk, held):
        part = pl.ds(chunk * CHUNK, CHUNK)
        intensity = jnp.dot(low_t[part, :], held, preferred_element_type=jnp.float32)
        return (data[part, :].astype(jnp.float32) / intensity).astype(jnp.bfloat16)

    numerator = jnp.zeros(old.shape, jnp.float32)
    for chunk in range(channels // CHUNK):
        ratios = ratios_of(chunk, old_low)
        numerator += jnp.dot(
            low[:, pl.ds(chunk * CHUNK, CHUNK)], ratios, preferred_element_type=jnp.float32
        )
    new = old * numerator / weight_den
    new_weights[...] = new
    new_low = new.astype(jnp.bfloat16)
    sums = jnp.sum(new[FIXED:], axis=1, keepdims=True)
    at = lax.broadcasted_iota(jnp.int32, (HALF, LANES), 0)
    lane = lax.broadcasted_iota(jnp.int32, (HALF, LANES), 1)
    den_rows = []
    for half in range(CORES):
        column = jnp.broadcast_to(sums[half * HALF : (half + 1) * HALF], (HALF, LANES))
        row = jnp.sum(jnp.where(at == lane, column, 0.0), axis=0, keepdims=True)
        den_rows.append(jnp.broadcast_to(row, (DEN_ROWS, LANES)))
    kept_row = jnp.where(first, den_rows[0], den_rows[1])
    sent_row = jnp.where(first, den_rows[1], den_rows[0])
    for chunk in range(channels // CHUNK):
        ratios = ratios_of(chunk, new_low)
        terms = lax.dot_general(
            new_low[FIXED:], ratios, (((1,), (1,)), ((), ())), preferred_element_type=jnp.float32
        )
        for part in range(CHUNK // LANES):
            shard = chunk * (CHUNK // LANES) + part
            upper = terms[:HALF, part * LANES : (part + 1) * LANES]
            lower = terms[HALF:, part * LANES : (part + 1) * LANES]
            kept[shard, :HALF] = jnp.where(first, upper, lower)
            sent[shard, :HALF] = jnp.where(first, lower, upper)
            kept[shard, HALF:] = kept_row
            sent[shard, HALF:] = sent_row


def update(core, data, template, own, other, weights):
    channels = data.shape[0]
    message = jax.ShapeDtypeStruct((channels // LANES, HALF + DEN_ROWS, LANES), jnp.float32)
    components = template.shape[0] + FREE
    return pl.pallas_call(
        update_kernel,
        out_shape=(jax.ShapeDtypeStruct(weights.shape, jnp.float32), message, message),
        in_specs=[SMEM, VMEM, VMEM, VMEM, VMEM, VMEM],
        out_specs=(VMEM, VMEM, VMEM),
        scratch_shapes=[
            pltpu.VMEM((components, channels), jnp.bfloat16),
            pltpu.VMEM((channels, components), jnp.bfloat16),
        ],
        compiler_params=pltpu.CompilerParams(vmem_limit_bytes=16 * 1024 * 1024),
        name="update",
    )(core, data, template, own, other, weights)


def whole_kernel(core, own, other, out):
    for half, blocks in ((core[0], own), (1 - core[0], other)):
        rows = pl.ds(pl.multiple_of(half * HALF, 8), HALF)
        for shard in range(blocks.shape[0]):
            out[rows, pl.ds(shard * LANES, LANES)] = blocks[shard]


def whole(core, own, other):
    return pl.pallas_call(
        whole_kernel,
        out_shape=jax.ShapeDtypeStruct((FREE, own.shape[0] * LANES), jnp.float32),
        in_specs=[SMEM, VMEM, VMEM],
        out_specs=VMEM,
        compiler_params=pltpu.CompilerParams(vmem_limit_bytes=4 * 1024 * 1024),
        name="whole",
    )(core, own, other)


def shards(counts, template_mask, weights_init, spectra_init):
    pixel_data = lax.all_to_all(smoothed(counts[0]), CHAN, split_axis=0, concat_axis=0, tiled=True)
    data = pixel_data.reshape(-1, pixel_data.shape[-1])
    core = lax.axis_index("core")
    template = template_mask.astype(jnp.bfloat16)
    weights = weights_init[0, 0]
    shard = lax.axis_index("y") * lax.axis_size("row") + lax.axis_index("row")
    halves = spectra_init.reshape(CORES, HALF, -1, LANES).transpose(0, 2, 1, 3)
    own, other = halves[core], halves[1 - core]
    own, other, block = lax.optimization_barrier((own, other, own[shard]))
    for iteration in range(ITERS):
        weights, kept, sent = update(core[None], data, template, own, other, weights)
        num, den = summed_block(kept, sent)
        block = block * num / den[:, None]
        own = to_all(block, PLANE)
        other = lax.ppermute(own, "core", [(0, 1), (1, 0)])
    return (weights[None, None], whole(core[None], own, other))


def solution(mesh):
    devices = np.asarray(mesh.devices)
    fine = jax.sharding.Mesh(devices.reshape(8, 4, 2, 4), ("z", "y", "core", "row"))
    placed = (P("row", None, CHAN, None), P(), P("row", CHAN, None, None), P())
    return jax.shard_map(
        shards,
        mesh=fine,
        in_specs=placed,
        out_specs=(P("row", CHAN, None, None), P()),
        check_vma=False,
    )
```

```python
import jax
import jax.numpy as jnp
import numpy as np
from jax import lax
from jax.experimental import pallas as pl
from jax.experimental.pallas import tpu as pltpu
from jax.sharding import PartitionSpec as P

FIXED = 32
FREE = 96
PASSES = 3
ITERS = 4
CHAN = ("z", "y", "core")
PLANE = ("y", "row")
CORES = 2
HALF = FREE // CORES
LANES = 128
DEN_ROWS = 8
CHUNK = 256
ROWS = 16
INNER_MIB = 60
EDGE_MIB = 53
TAU = 8.0 / 3.0
SCALE = 0.15**3
VMEM = pl.BlockSpec(memory_space=pltpu.VMEM)
SMEM = pl.BlockSpec(memory_space=pltpu.SMEM)
HBM = pl.BlockSpec(memory_space=pltpu.HBM)


def column_sums(width):
    row = lax.broadcasted_iota(jnp.int32, (width, width), 0)
    column = lax.broadcasted_iota(jnp.int32, (width, width), 1)
    apart, total = jnp.abs(row - column), row + column
    corner = (total == 0) | (total == 2 * width - 2)
    beside_corner = (total == 1) | (total == 2 * width - 3)
    first = jnp.where(apart == 1, 3.0, 0.0)
    second = jnp.where(apart == 2, 3.0, jnp.where(apart == 0, jnp.where(corner, 3.0, 6.0), 0.0))
    third = jnp.where(apart == 3, 1.0, jnp.where(apart == 1, jnp.where(beside_corner, 2.0, 3.0), 0.0))
    return [power.astype(jnp.bfloat16) for power in (first, second, third)]


def fill_sums(sums):
    width = sums.shape[0]
    for at, power in enumerate(column_sums(width)):
        sums[:, pl.ds(at * width, width)] = power


def beside_of(rows, sums):
    width = rows.shape[-1]
    flat = rows.reshape(-1, width).astype(jnp.bfloat16)
    out = jnp.dot(flat, sums, preferred_element_type=jnp.float32)
    return [out[:, at * width : (at + 1) * width].reshape(rows.shape) for at in range(PASSES)]


def inner_kernel(counts, out, sums, held, plain, beside, once, twice, done, in_sem, out_sem):
    lines = counts.shape[0]
    turns = lines // ROWS

    def fetch(turn):
        rows = pl.ds(turn * ROWS, ROWS)
        return pltpu.make_async_copy(counts.at[rows], held.at[rows], in_sem.at[turn])

    def ship(turn):
        start = turn * ROWS - PASSES
        return pltpu.make_async_copy(
            done.at[pl.ds(start + ROWS, ROWS)], out.at[pl.ds(start, ROWS)], out_sem.at[turn]
        )

    for turn in range(turns):
        fetch(turn).start()
    fill_sums(sums)

    for turn in range(turns):
        fetch(turn).wait()
        base = turn * ROWS
        x = held[pl.ds(base, ROWS)].astype(jnp.float32)
        plain[pl.ds(base + ROWS, ROWS)] = x
        for at, value in enumerate(beside_of(x, sums[...])):
            beside[at, pl.ds(base + ROWS, ROWS)] = value
        for step, (source, target) in enumerate(((plain, once), (once, twice), (twice, done))):
            for row in range(ROWS):
                at = base + ROWS + row - step - 1
                value = TAU * source[at] + (source[at - 1] + source[at + 1]) + beside[step, at]
                if step == PASSES - 1:
                    value = (SCALE * value).astype(jnp.bfloat16)
                target[at] = value

        if turn:
            ship(turn).start()

    short = pltpu.make_async_copy(
        done.at[pl.ds(ROWS + PASSES, ROWS - 2 * PASSES)], out.at[pl.ds(PASSES, ROWS - 2 * PASSES)], out_sem.at[0]
    )
    short.start()
    short.wait()
    for turn in range(1, turns):
        ship(turn).wait()


def edge_kernel(flags, counts, before, after, inner, out, sums, near, rim, ends, in_sem, sem):
    del inner
    lines = out.shape[0]
    rows = 2 * PASSES
    fetches = [
        pltpu.make_async_copy(counts.at[pl.ds(0, rows)], near.at[0], in_sem.at[0]),
        pltpu.make_async_copy(counts.at[pl.ds(lines - rows, rows)], near.at[1], in_sem.at[1]),
        pltpu.make_async_copy(before, rim.at[0], in_sem.at[2]),
        pltpu.make_async_copy(after, rim.at[1], in_sem.at[3]),
    ]
    for fetch in fetches:
        fetch.start()
    fill_sums(sums)
    for fetch in fetches:
        fetch.wait()
    copies = []
    for top in (True, False):
        side = 0 if top else 1
        own, beyond = near[side].astype(jnp.float32), rim[side].astype(jnp.float32)
        pair = (beyond, own) if top else (own, beyond)
        field = jnp.concatenate(pair, axis=0)
        beside = []
        for step in range(PASSES):
            power = sums[:, pl.ds(step * field.shape[-1], field.shape[-1])]
            part = field[1 + step : 3 * PASSES - 1 - step]
            flat = part.reshape(-1, part.shape[-1]).astype(jnp.bfloat16)
            beside.append(jnp.dot(flat, power, preferred_element_type=jnp.float32).reshape(part.shape))
        rows = [field[row] for row in range(3 * PASSES)]
        flag = flags[0] if top else flags[1]
        for step in range(PASSES):
            rows = [
                TAU * rows[row + 1] + (rows[row] + rows[row + 2]) + beside[step][row]
                for row in range(len(rows) - 2)
            ]
            beyond = PASSES - 1 - step
            for row in range(beyond):
                spot = row if top else len(rows) - 1 - row
                rows[spot] = rows[spot] * flag
        for row in range(PASSES):
            ends[side, row] = (SCALE * rows[row]).astype(jnp.bfloat16)
        target = out.at[pl.ds(0 if top else lines - PASSES, PASSES)]
        copies.append(pltpu.make_async_copy(ends.at[side], target, sem.at[side]))
        copies[-1].start()
    for copy in copies:
        copy.wait()


def smoothed(counts):
    lines, channels, width = counts.shape
    size, row = lax.axis_size("row"), lax.axis_index("row")
    up = [(i, i + 1) for i in range(size - 1)]
    down = [(j, i) for i, j in up]
    first, last = lax.optimization_barrier((counts[:PASSES], counts[-PASSES:]))
    before = lax.ppermute(last.astype(jnp.bfloat16), "row", up)
    after = lax.ppermute(first.astype(jnp.bfloat16), "row", down)
    flags = jnp.stack([row > 0, row < size - 1]).astype(jnp.float32)
    shape = jax.ShapeDtypeStruct(counts.shape, jnp.bfloat16)
    padded = (lines + 2 * ROWS, channels, width)
    sums = pltpu.VMEM((width, PASSES * width), jnp.bfloat16)
    inner = pl.pallas_call(
        inner_kernel,
        out_shape=shape,
        in_specs=[HBM],
        out_specs=HBM,
        scratch_shapes=[
            sums,
            pltpu.VMEM(counts.shape, jnp.int32),
            pltpu.VMEM(padded, jnp.float32),
            pltpu.VMEM((PASSES,) + padded, jnp.float32),
            pltpu.VMEM(padded, jnp.float32),
            pltpu.VMEM(padded, jnp.float32),
            pltpu.VMEM(padded, jnp.bfloat16),
            pltpu.SemaphoreType.DMA((lines // ROWS,)),
            pltpu.SemaphoreType.DMA((lines // ROWS,)),
        ],
        compiler_params=pltpu.CompilerParams(vmem_limit_bytes=INNER_MIB * 1024 * 1024),
        cost_estimate=pl.CostEstimate(
            flops=2 * lines * channels * width * width, bytes_accessed=6 * lines * channels * width, transcendentals=0
        ),
        name="smooth_inner",
    )(counts)
    return pl.pallas_call(
        edge_kernel,
        out_shape=shape,
        in_specs=[SMEM, HBM, HBM, HBM, HBM],
        out_specs=HBM,
        scratch_shapes=[
            sums,
            pltpu.VMEM((2, 2 * PASSES, channels, width), jnp.int32),
            pltpu.VMEM((2, PASSES, channels, width), jnp.bfloat16),
            pltpu.VMEM((2, PASSES, channels, width), jnp.bfloat16),
            pltpu.SemaphoreType.DMA((4,)),
            pltpu.SemaphoreType.DMA((2,)),
        ],
        input_output_aliases={4: 0},
        compiler_params=pltpu.CompilerParams(vmem_limit_bytes=EDGE_MIB * 1024 * 1024),
        name="smooth_edges",
    )(flags, counts, before, after, inner)


def to_all(x, axes):
    count = 1
    for axis in axes:
        count *= lax.axis_size(axis)
    return lax.all_to_all(jnp.broadcast_to(x[None], (count,) + x.shape), axes, 0, 0, tiled=True)


def summed_block(kept, sent):
    chip = kept + lax.ppermute(sent, "core", [(0, 1), (1, 0)])
    plane = jnp.sum(lax.all_to_all(chip, PLANE, 0, 0, tiled=True), axis=0)
    total = jnp.sum(to_all(plane, ("z",)), axis=0)
    return total[:HALF], total[HALF, :HALF]


def update_kernel(core, data, template, own, other, weights, new_weights, kept, sent, low, low_t):
    channels, pixels = data.shape
    shards = channels // LANES
    mine = core[0]
    first = mine == 0
    den = []
    low[:FIXED] = template[...]
    for half, blocks in ((mine, own), (1 - mine, other)):
        rows = pl.ds(pl.multiple_of(FIXED + half * HALF, 16), HALF)
        total = jnp.zeros((HALF, LANES), jnp.float32)
        for shard in range(shards):
            part = blocks[shard]
            total = total + part
            low[rows, pl.ds(shard * LANES, LANES)] = part.astype(jnp.bfloat16)
        den.append(jnp.sum(total, axis=1, keepdims=True))
    upper, lower = jnp.where(first, den[0], den[1]), jnp.where(first, den[1], den[0])
    fixed = jnp.sum(template[...].astype(jnp.float32), axis=1, keepdims=True)
    weight_den = jnp.concatenate([fixed, upper, lower], axis=0)
    for shard in range(shards):
        low_t[pl.ds(shard * LANES, LANES), :] = low[:, pl.ds(shard * LANES, LANES)].T

    old = weights[...]
    old_low = old.astype(jnp.bfloat16)

    def ratios_of(chunk, held):
        part = pl.ds(chunk * CHUNK, CHUNK)
        intensity = jnp.dot(low_t[part, :], held, preferred_element_type=jnp.float32)
        return (data[part, :].astype(jnp.float32) / intensity).astype(jnp.bfloat16)

    numerator = jnp.zeros(old.shape, jnp.float32)
    for chunk in range(channels // CHUNK):
        ratios = ratios_of(chunk, old_low)
        numerator += jnp.dot(
            low[:, pl.ds(chunk * CHUNK, CHUNK)], ratios, preferred_element_type=jnp.float32
        )
    new = old * numerator / weight_den
    new_weights[...] = new
    new_low = new.astype(jnp.bfloat16)
    sums = jnp.sum(new[FIXED:], axis=1, keepdims=True)
    at = lax.broadcasted_iota(jnp.int32, (HALF, LANES), 0)
    lane = lax.broadcasted_iota(jnp.int32, (HALF, LANES), 1)
    den_rows = []
    for half in range(CORES):
        column = jnp.broadcast_to(sums[half * HALF : (half + 1) * HALF], (HALF, LANES))
        row = jnp.sum(jnp.where(at == lane, column, 0.0), axis=0, keepdims=True)
        den_rows.append(jnp.broadcast_to(row, (DEN_ROWS, LANES)))
    kept_row = jnp.where(first, den_rows[0], den_rows[1])
    sent_row = jnp.where(first, den_rows[1], den_rows[0])
    for chunk in range(channels // CHUNK):
        ratios = ratios_of(chunk, new_low)
        terms = lax.dot_general(
            new_low[FIXED:], ratios, (((1,), (1,)), ((), ())), preferred_element_type=jnp.float32
        )
        for part in range(CHUNK // LANES):
            shard = chunk * (CHUNK // LANES) + part
            upper = terms[:HALF, part * LANES : (part + 1) * LANES]
            lower = terms[HALF:, part * LANES : (part + 1) * LANES]
            kept[shard, :HALF] = jnp.where(first, upper, lower)
            sent[shard, :HALF] = jnp.where(first, lower, upper)
            kept[shard, HALF:] = kept_row
            sent[shard, HALF:] = sent_row


def update(core, data, template, own, other, weights):
    channels = data.shape[0]
    message = jax.ShapeDtypeStruct((channels // LANES, HALF + DEN_ROWS, LANES), jnp.float32)
    components = template.shape[0] + FREE
    return pl.pallas_call(
        update_kernel,
        out_shape=(jax.ShapeDtypeStruct(weights.shape, jnp.float32), message, message),
        in_specs=[SMEM, VMEM, VMEM, VMEM, VMEM, VMEM],
        out_specs=(VMEM, VMEM, VMEM),
        scratch_shapes=[
            pltpu.VMEM((components, channels), jnp.bfloat16),
            pltpu.VMEM((channels, components), jnp.bfloat16),
        ],
        compiler_params=pltpu.CompilerParams(vmem_limit_bytes=16 * 1024 * 1024),
        name="update",
    )(core, data, template, own, other, weights)


def whole_kernel(core, own, other, out):
    for half, blocks in ((core[0], own), (1 - core[0], other)):
        rows = pl.ds(pl.multiple_of(half * HALF, 8), HALF)
        for shard in range(blocks.shape[0]):
            out[rows, pl.ds(shard * LANES, LANES)] = blocks[shard]


def whole(core, own, other):
    return pl.pallas_call(
        whole_kernel,
        out_shape=jax.ShapeDtypeStruct((FREE, own.shape[0] * LANES), jnp.float32),
        in_specs=[SMEM, VMEM, VMEM],
        out_specs=VMEM,
        compiler_params=pltpu.CompilerParams(vmem_limit_bytes=4 * 1024 * 1024),
        name="whole",
    )(core, own, other)


def shards(counts, template_mask, weights_init, spectra_init):
    pixel_data = lax.all_to_all(smoothed(counts[0]), CHAN, split_axis=0, concat_axis=0, tiled=True)
    data = pixel_data.reshape(-1, pixel_data.shape[-1])
    core = lax.axis_index("core")
    template = template_mask.astype(jnp.bfloat16)
    weights = weights_init[0, 0]
    shard = lax.axis_index("y") * lax.axis_size("row") + lax.axis_index("row")
    halves = spectra_init.reshape(CORES, HALF, -1, LANES).transpose(0, 2, 1, 3)
    own, other = halves[core], halves[1 - core]
    own, other, block = lax.optimization_barrier((own, other, own[shard]))
    for iteration in range(ITERS):
        weights, kept, sent = update(core[None], data, template, own, other, weights)
        num, den = summed_block(kept, sent)
        block = block * num / den[:, None]
        own = to_all(block, PLANE)
        other = lax.ppermute(own, "core", [(0, 1), (1, 0)])
    return (weights[None, None], whole(core[None], own, other))


def solution(mesh):
    devices = np.asarray(mesh.devices)
    fine = jax.sharding.Mesh(devices.reshape(8, 4, 2, 4), ("z", "y", "core", "row"))
    placed = (P("row", None, CHAN, None), P(), P("row", CHAN, None, None), P())
    return jax.shard_map(
        shards,
        mesh=fine,
        in_specs=placed,
        out_specs=(P("row", CHAN, None, None), P()),
        check_vma=False,
    )
```

```python
import jax
import jax.numpy as jnp
import numpy as np
from jax import lax
from jax.experimental import pallas as pl
from jax.experimental.pallas import tpu as pltpu
from jax.sharding import PartitionSpec as P

FIXED = 32
FREE = 96
PASSES = 3
ITERS = 4
CHAN = ("z", "y", "core")
PLANE = ("y", "row")
CORES = 2
HALF = FREE // CORES
LANES = 128
DEN_ROWS = 8
CHUNK = 512
ROWS = 8
INNER_MIB = 60
EDGE_MIB = 53
TAU = 8.0 / 3.0
SCALE = 0.15**3
VMEM = pl.BlockSpec(memory_space=pltpu.VMEM)
SMEM = pl.BlockSpec(memory_space=pltpu.SMEM)
HBM = pl.BlockSpec(memory_space=pltpu.HBM)


def column_sums(width):
    row = lax.broadcasted_iota(jnp.int32, (width, width), 0)
    column = lax.broadcasted_iota(jnp.int32, (width, width), 1)
    apart, total = jnp.abs(row - column), row + column
    corner = (total == 0) | (total == 2 * width - 2)
    beside_corner = (total == 1) | (total == 2 * width - 3)
    first = jnp.where(apart == 1, 3.0, 0.0)
    second = jnp.where(apart == 2, 3.0, jnp.where(apart == 0, jnp.where(corner, 3.0, 6.0), 0.0))
    third = jnp.where(apart == 3, 1.0, jnp.where(apart == 1, jnp.where(beside_corner, 2.0, 3.0), 0.0))
    return [power.astype(jnp.bfloat16) for power in (first, second, third)]


def fill_sums(sums):
    width = sums.shape[0]
    for at, power in enumerate(column_sums(width)):
        sums[:, pl.ds(at * width, width)] = power


def beside_of(rows, sums):
    width = rows.shape[-1]
    flat = rows.reshape(-1, width).astype(jnp.bfloat16)
    out = jnp.dot(flat, sums, preferred_element_type=jnp.float32)
    return [out[:, at * width : (at + 1) * width].reshape(rows.shape) for at in range(PASSES)]


def inner_kernel(counts, out, sums, held, plain, beside, once, twice, done, in_sem, out_sem):
    lines = counts.shape[0]
    turns = lines // ROWS

    def fetch(turn):
        rows = pl.ds(turn * ROWS, ROWS)
        return pltpu.make_async_copy(counts.at[rows], held.at[rows], in_sem.at[turn])

    def ship(turn):
        start = turn * ROWS - PASSES
        return pltpu.make_async_copy(
            done.at[pl.ds(start + ROWS, ROWS)], out.at[pl.ds(start, ROWS)], out_sem.at[turn]
        )

    for turn in range(turns):
        fetch(turn).start()
    fill_sums(sums)

    for turn in range(turns):
        fetch(turn).wait()
        base = turn * ROWS
        x = held[pl.ds(base, ROWS)].astype(jnp.float32)
        plain[pl.ds(base + ROWS, ROWS)] = x
        for at, value in enumerate(beside_of(x, sums[...])):
            beside[at, pl.ds(base + ROWS, ROWS)] = value
        for step, (source, target) in enumerate(((plain, once), (once, twice), (twice, done))):
            for row in range(ROWS):
                at = base + ROWS + row - step - 1
                value = TAU * source[at] + (source[at - 1] + source[at + 1]) + beside[step, at]
                if step == PASSES - 1:
                    value = (SCALE * value).astype(jnp.bfloat16)
                target[at] = value

        if turn:
            ship(turn).start()

    short = pltpu.make_async_copy(
        done.at[pl.ds(ROWS + PASSES, ROWS - 2 * PASSES)], out.at[pl.ds(PASSES, ROWS - 2 * PASSES)], out_sem.at[0]
    )
    short.start()
    short.wait()
    for turn in range(1, turns):
        ship(turn).wait()


def edge_kernel(flags, counts, before, after, inner, out, sums, near, rim, ends, in_sem, sem):
    del inner
    lines = out.shape[0]
    rows = 2 * PASSES
    fetches = [
        pltpu.make_async_copy(counts.at[pl.ds(0, rows)], near.at[0], in_sem.at[0]),
        pltpu.make_async_copy(counts.at[pl.ds(lines - rows, rows)], near.at[1], in_sem.at[1]),
        pltpu.make_async_copy(before, rim.at[0], in_sem.at[2]),
        pltpu.make_async_copy(after, rim.at[1], in_sem.at[3]),
    ]
    for fetch in fetches:
        fetch.start()
    fill_sums(sums)
    for fetch in fetches:
        fetch.wait()
    copies = []
    for top in (True, False):
        side = 0 if top else 1
        own, beyond = near[side].astype(jnp.float32), rim[side].astype(jnp.float32)
        pair = (beyond, own) if top else (own, beyond)
        field = jnp.concatenate(pair, axis=0)
        beside = beside_of(field, sums[...])
        rows = [field[row] for row in range(3 * PASSES)]
        flag = flags[0] if top else flags[1]
        for step in range(PASSES):
            rows = [
                TAU * rows[row + 1] + (rows[row] + rows[row + 2]) + beside[step][row + 1 + step]
                for row in range(len(rows) - 2)
            ]
            beyond = PASSES - 1 - step
            for row in range(beyond):
                spot = row if top else len(rows) - 1 - row
                rows[spot] = rows[spot] * flag
        for row in range(PASSES):
            ends[side, row] = (SCALE * rows[row]).astype(jnp.bfloat16)
        target = out.at[pl.ds(0 if top else lines - PASSES, PASSES)]
        copies.append(pltpu.make_async_copy(ends.at[side], target, sem.at[side]))
        copies[-1].start()
    for copy in copies:
        copy.wait()


def smoothed(counts):
    lines, channels, width = counts.shape
    size, row = lax.axis_size("row"), lax.axis_index("row")
    up = [(i, i + 1) for i in range(size - 1)]
    down = [(j, i) for i, j in up]
    first, last = lax.optimization_barrier((counts[:PASSES], counts[-PASSES:]))
    before = lax.ppermute(last.astype(jnp.bfloat16), "row", up)
    after = lax.ppermute(first.astype(jnp.bfloat16), "row", down)
    flags = jnp.stack([row > 0, row < size - 1]).astype(jnp.float32)
    shape = jax.ShapeDtypeStruct(counts.shape, jnp.bfloat16)
    padded = (lines + 2 * ROWS, channels, width)
    sums = pltpu.VMEM((width, PASSES * width), jnp.bfloat16)
    inner = pl.pallas_call(
        inner_kernel,
        out_shape=shape,
        in_specs=[HBM],
        out_specs=HBM,
        scratch_shapes=[
            sums,
            pltpu.VMEM(counts.shape, jnp.int32),
            pltpu.VMEM(padded, jnp.float32),
            pltpu.VMEM((PASSES,) + padded, jnp.float32),
            pltpu.VMEM(padded, jnp.float32),
            pltpu.VMEM(padded, jnp.float32),
            pltpu.VMEM(padded, jnp.bfloat16),
            pltpu.SemaphoreType.DMA((lines // ROWS,)),
            pltpu.SemaphoreType.DMA((lines // ROWS,)),
        ],
        compiler_params=pltpu.CompilerParams(vmem_limit_bytes=INNER_MIB * 1024 * 1024),
        cost_estimate=pl.CostEstimate(
            flops=2 * lines * channels * width * width, bytes_accessed=6 * lines * channels * width, transcendentals=0
        ),
        name="smooth_inner",
    )(counts)
    return pl.pallas_call(
        edge_kernel,
        out_shape=shape,
        in_specs=[SMEM, HBM, HBM, HBM, HBM],
        out_specs=HBM,
        scratch_shapes=[
            sums,
            pltpu.VMEM((2, 2 * PASSES, channels, width), jnp.int32),
            pltpu.VMEM((2, PASSES, channels, width), jnp.bfloat16),
            pltpu.VMEM((2, PASSES, channels, width), jnp.bfloat16),
            pltpu.SemaphoreType.DMA((4,)),
            pltpu.SemaphoreType.DMA((2,)),
        ],
        input_output_aliases={4: 0},
        compiler_params=pltpu.CompilerParams(vmem_limit_bytes=EDGE_MIB * 1024 * 1024),
        name="smooth_edges",
    )(flags, counts, before, after, inner)


def to_all(x, axes):
    count = 1
    for axis in axes:
        count *= lax.axis_size(axis)
    return lax.all_to_all(jnp.broadcast_to(x[None], (count,) + x.shape), axes, 0, 0, tiled=True)


def summed_block(kept, sent):
    chip = kept + lax.ppermute(sent, "core", [(0, 1), (1, 0)])
    plane = jnp.sum(lax.all_to_all(chip, PLANE, 0, 0, tiled=True), axis=0)
    total = jnp.sum(to_all(plane, ("z",)), axis=0)
    return total[:HALF], total[HALF, :HALF]


def update_kernel(core, data, template, own, other, weights, new_weights, kept, sent, low, low_t):
    channels, pixels = data.shape
    shards = channels // LANES
    mine = core[0]
    first = mine == 0
    den = []
    low[:FIXED] = template[...]
    for half, blocks in ((mine, own), (1 - mine, other)):
        rows = pl.ds(pl.multiple_of(FIXED + half * HALF, 16), HALF)
        total = jnp.zeros((HALF, LANES), jnp.float32)
        for shard in range(shards):
            part = blocks[shard]
            total = total + part
            low[rows, pl.ds(shard * LANES, LANES)] = part.astype(jnp.bfloat16)
        den.append(jnp.sum(total, axis=1, keepdims=True))
    upper, lower = jnp.where(first, den[0], den[1]), jnp.where(first, den[1], den[0])
    fixed = jnp.sum(template[...].astype(jnp.float32), axis=1, keepdims=True)
    weight_den = jnp.concatenate([fixed, upper, lower], axis=0)
    for shard in range(shards):
        low_t[pl.ds(shard * LANES, LANES), :] = low[:, pl.ds(shard * LANES, LANES)].T

    old = weights[...]
    old_low = old.astype(jnp.bfloat16)

    def ratios_of(chunk, held):
        part = pl.ds(chunk * CHUNK, CHUNK)
        intensity = jnp.dot(low_t[part, :], held, preferred_element_type=jnp.float32)
        return (data[part, :].astype(jnp.float32) / intensity).astype(jnp.bfloat16)

    numerator = jnp.zeros(old.shape, jnp.float32)
    for chunk in range(channels // CHUNK):
        ratios = ratios_of(chunk, old_low)
        numerator += jnp.dot(
            low[:, pl.ds(chunk * CHUNK, CHUNK)], ratios, preferred_element_type=jnp.float32
        )
    new = old * numerator / weight_den
    new_weights[...] = new
    new_low = new.astype(jnp.bfloat16)
    sums = jnp.sum(new[FIXED:], axis=1, keepdims=True)
    at = lax.broadcasted_iota(jnp.int32, (HALF, LANES), 0)
    lane = lax.broadcasted_iota(jnp.int32, (HALF, LANES), 1)
    den_rows = []
    for half in range(CORES):
        column = jnp.broadcast_to(sums[half * HALF : (half + 1) * HALF], (HALF, LANES))
        row = jnp.sum(jnp.where(at == lane, column, 0.0), axis=0, keepdims=True)
        den_rows.append(jnp.broadcast_to(row, (DEN_ROWS, LANES)))
    kept_row = jnp.where(first, den_rows[0], den_rows[1])
    sent_row = jnp.where(first, den_rows[1], den_rows[0])
    for chunk in range(channels // CHUNK):
        ratios = ratios_of(chunk, new_low)
        terms = lax.dot_general(
            new_low[FIXED:], ratios, (((1,), (1,)), ((), ())), preferred_element_type=jnp.float32
        )
        for part in range(CHUNK // LANES):
            shard = chunk * (CHUNK // LANES) + part
            upper = terms[:HALF, part * LANES : (part + 1) * LANES]
            lower = terms[HALF:, part * LANES : (part + 1) * LANES]
            kept[shard, :HALF] = jnp.where(first, upper, lower)
            sent[shard, :HALF] = jnp.where(first, lower, upper)
            kept[shard, HALF:] = kept_row
            sent[shard, HALF:] = sent_row


def update(core, data, template, own, other, weights):
    channels = data.shape[0]
    message = jax.ShapeDtypeStruct((channels // LANES, HALF + DEN_ROWS, LANES), jnp.float32)
    components = template.shape[0] + FREE
    return pl.pallas_call(
        update_kernel,
        out_shape=(jax.ShapeDtypeStruct(weights.shape, jnp.float32), message, message),
        in_specs=[SMEM, VMEM, VMEM, VMEM, VMEM, VMEM],
        out_specs=(VMEM, VMEM, VMEM),
        scratch_shapes=[
            pltpu.VMEM((components, channels), jnp.bfloat16),
            pltpu.VMEM((channels, components), jnp.bfloat16),
        ],
        compiler_params=pltpu.CompilerParams(vmem_limit_bytes=16 * 1024 * 1024),
        name="update",
    )(core, data, template, own, other, weights)


def whole_kernel(core, own, other, out):
    for half, blocks in ((core[0], own), (1 - core[0], other)):
        rows = pl.ds(pl.multiple_of(half * HALF, 8), HALF)
        for shard in range(blocks.shape[0]):
            out[rows, pl.ds(shard * LANES, LANES)] = blocks[shard]


def whole(core, own, other):
    return pl.pallas_call(
        whole_kernel,
        out_shape=jax.ShapeDtypeStruct((FREE, own.shape[0] * LANES), jnp.float32),
        in_specs=[SMEM, VMEM, VMEM],
        out_specs=VMEM,
        compiler_params=pltpu.CompilerParams(vmem_limit_bytes=4 * 1024 * 1024),
        name="whole",
    )(core, own, other)


def shards(counts, template_mask, weights_init, spectra_init):
    pixel_data = lax.all_to_all(smoothed(counts[0]), CHAN, split_axis=0, concat_axis=0, tiled=True)
    data = pixel_data.reshape(-1, pixel_data.shape[-1])
    core = lax.axis_index("core")
    template = template_mask.astype(jnp.bfloat16)
    weights = weights_init[0, 0]
    shard = lax.axis_index("y") * lax.axis_size("row") + lax.axis_index("row")
    halves = spectra_init.reshape(CORES, HALF, -1, LANES).transpose(0, 2, 1, 3)
    own, other = halves[core], halves[1 - core]
    own, other, block = lax.optimization_barrier((own, other, own[shard]))
    for iteration in range(ITERS):
        weights, kept, sent = update(core[None], data, template, own, other, weights)
        num, den = summed_block(kept, sent)
        block = block * num / den[:, None]
        own = to_all(block, PLANE)
        other = lax.ppermute(own, "core", [(0, 1), (1, 0)])
    return (weights[None, None], whole(core[None], own, other))


def solution(mesh):
    devices = np.asarray(mesh.devices)
    fine = jax.sharding.Mesh(devices.reshape(8, 4, 2, 4), ("z", "y", "core", "row"))
    placed = (P("row", None, CHAN, None), P(), P("row", CHAN, None, None), P())
    return jax.shard_map(
        shards,
        mesh=fine,
        in_specs=placed,
        out_specs=(P("row", CHAN, None, None), P()),
        check_vma=False,
    )
```
